256 devices in a mesh: hid: 32 (over z, y), wid: 8 (over x, core).
Axes of the slice: x: 4, y: 4, z: 8, core: 2. Of those that a mesh axis runs over, the one named last changes fastest.
Arguments:
- tokens: bfloat16 [1280, 16384], P('hid', 'wid'), may hold values from -6 to 6
- gate_first: bfloat16 [12288, 16384], P('hid', 'wid'), may hold values from -0.0625 to 0.0625
- up_first: bfloat16 [12288, 16384], P('hid', 'wid'), may hold values from -0.0625 to 0.0625
- down_first: bfloat16 [12288, 16384], P('hid', 'wid'), may hold values from -0.078125 to 0.078125
- gate_second: bfloat16 [12288, 16384], P('hid', 'wid'), may hold values from -0.0625 to 0.0625
- up_second: bfloat16 [12288, 16384], P('hid', 'wid'), may hold values from -0.0625 to 0.0625
- down_second: bfloat16 [12288, 16384], P('hid', 'wid'), may hold values from -0.078125 to 0.078125
- unit_order: int32 [12288], replicated, may hold values from 0 to 12287, as said below
Outputs:
- mixed: bfloat16 [1280, 16384], P('hid', 'wid')
The draws below stay inside these ranges and needn't reach their ends.
Inputs may be any that keep to these rules, and one draw needn't show every extreme that they name: `unit_order`: A permutation of the 12288 hidden units. Cut into 32 aligned blocks of 384 entries; block d holds at most 24 values from any one block s (values s * 384 to (s + 1) * 384 - 1), and exactly 24 for some pairs.
All inputs are finite; a program needn't handle non-finite values.
Results may differ from the reference program's by a relative error of at most 0.0049.
Values may be sent and summed in bfloat16 or wider, within the bound.
No kernel may reach another device: no remote copies, remote signals or barrier semaphores. Data moves between devices by JAX's collectives and lax.ppermute only.
A program may use at most 128 MiB of HBM per device.

```python
import jax
import jax.numpy as jnp
from jax import lax

D = 16384
H = 12288
TOKENS = 1280
R = 384
CAP = 24


def draw_unit_order(key, part):
    key = jax.random.fold_in(key, 7)
    key_list = jax.random.split(key, 5)
    groups = H // R
    lane_rows = CAP // 2
    offsets = jax.random.permutation(key_list[0], groups)
    lane_ids = jnp.arange(groups)
    half_lanes = groups // 2
    quarter_lanes = groups // 4
    lane_pick = jnp.where(lane_ids < half_lanes, lane_ids // 2, quarter_lanes + lane_ids - half_lanes)
    shifts = offsets[lane_pick]
    outer_map = jax.random.permutation(key_list[1], groups)
    inner_map = jax.random.permutation(key_list[2], groups)
    outer_back = jnp.argsort(outer_map)
    inner_back = jnp.argsort(inner_map)
    base_rows = jnp.broadcast_to(jnp.arange(R, dtype=jnp.int32)[None, :], (groups, R))
    source_order = jax.random.permutation(key_list[3], base_rows, axis=1, independent=True)
    target_order = jax.random.permutation(key_list[4], base_rows, axis=1, independent=True)
    dest_dev = jnp.arange(groups)[:, None, None]
    lane_grid = lane_ids[None, :, None]
    within_lane = jnp.arange(lane_rows)[None, None, :]
    source = inner_back[(outer_back[dest_dev] - shifts[lane_grid]) % groups]
    slot_ids = lane_grid * lane_rows + within_lane
    values = source * R + source_order[source, slot_ids]
    places = dest_dev * R + target_order[dest_dev, slot_ids]
    result = jnp.zeros((H,), jnp.int32).at[places.reshape(-1)].set(values.reshape(-1).astype(jnp.int32))
    return result.astype(jnp.int32)


def level_of(rng, extent, shards, low, largest):
    def one(axis_at, shards_of):
        heights = jax.random.uniform(jax.random.fold_in(jax.random.fold_in(rng, 6), axis_at), (shards_of,), jnp.float32, low / len(shards), largest / len(shards))
        return jnp.repeat(jnp.exp(heights), extent[axis_at] // shards_of).reshape((-1,) + (1,) * (len(extent) - axis_at - 1))

    level = one(*shards[0])
    for cut in shards[1:]:
        level = level * one(*cut)
    return level


def noise(key, shape, deviation, limit, shards=(), held_as=jnp.bfloat16):
    factor_of = level_of(key, shape, shards, -0.22, 0.18) if shards else 1.0
    entries = jax.random.normal(key, shape, jnp.float32) * deviation * factor_of
    return jnp.minimum(jnp.maximum(entries, -limit), limit).astype(held_as)


def setup_inputs(seed: int = 0) -> dict:
    seeds = jax.random.split(jax.random.key(seed), 9)
    tokens = noise(seeds[0], (TOKENS, D), 1.0, 6.0, ((0, 32), (1, 8)))
    gate_first = noise(seeds[1], (H, D), (D // 2) ** -0.5, 0.0625, ((0, 32), (1, 8)))
    up_first = noise(seeds[2], (H, D), (D // 2) ** -0.5, 0.0625, ((0, 32), (1, 8)))
    down_first = noise(seeds[3], (H, D), (H // 2) ** -0.5, 0.078125, ((0, 32), (1, 8)))
    gate_second = noise(seeds[4], (H, D), (D // 2) ** -0.5, 0.0625, ((0, 32), (1, 8)))
    up_second = noise(seeds[5], (H, D), (D // 2) ** -0.5, 0.0625, ((0, 32), (1, 8)))
    down_second = noise(seeds[6], (H, D), (H // 2) ** -0.5, 0.078125, ((0, 32), (1, 8)))
    unit_order = draw_unit_order(jax.random.fold_in(seeds[8], 71), 0)
    return {"tokens": tokens, "gate_first": gate_first, "up_first": up_first, "down_first": down_first, "gate_second": gate_second, "up_second": up_second, "down_second": down_second, "unit_order": unit_order}


def product_rows(left, right):
    return lax.dot_general(left, right, (((1,), (1,)), ((), ())), preferred_element_type=jnp.float32)


def reference(tokens, gate_first, up_first, down_first, gate_second, up_second, down_second, unit_order):
    gate_moved = jnp.take(gate_second, unit_order, axis=0)
    up_moved = jnp.take(up_second, unit_order, axis=0)
    down_moved = jnp.take(down_second, unit_order, axis=0)
    gate = (product_rows(tokens, gate_first) + product_rows(tokens, gate_moved)) * 0.5
    up = (product_rows(tokens, up_first) + product_rows(tokens, up_moved)) * 0.5
    hidden = (jax.nn.silu(gate) * up).astype(jnp.bfloat16)
    first_term = jnp.dot(hidden, down_first, preferred_element_type=jnp.float32)
    second_term = jnp.dot(hidden, down_moved, preferred_element_type=jnp.float32)
    return ((first_term + second_term) * 0.5).astype(jnp.bfloat16)
```

```python
import jax
import jax.numpy as jnp
from jax import lax
from jax.sharding import Mesh, PartitionSpec as P

F32 = jnp.float32
BF16 = jnp.bfloat16
SIZES = {"z": 8, "y": 4, "x": 4, "c": 2}


def product(left, right, axis):
    return lax.dot_general(left, right, (((axis,), (axis,)), ((), ())), preferred_element_type=F32)


def shift(value, axis, step):
    size = SIZES[axis]
    return lax.ppermute(value, axis, [(i, (i + step) % size) for i in range(size)])


def ring_gather(block, axis):
    size = SIZES[axis]
    me = lax.axis_index(axis)
    rows, cols = block.shape
    out = jnp.zeros((size, rows, cols), block.dtype)

    def put(out, value, offset, col):
        return lax.dynamic_update_slice(out, value[None], ((me + offset + size) % size, 0, col))

    out = put(out, block, 0, 0)
    right = left = block
    for step in range(1, size // 2):
        right = shift(right, axis, 1)
        left = shift(left, axis, -1)
        out = put(out, right, -step, 0)
        out = put(out, left, step, 0)
    half = cols // 2
    first = shift(right[:, :half], axis, 1)
    second = shift(left[:, half:], axis, -1)
    out = put(out, first, size // 2, 0)
    out = put(out, second, size // 2, half)
    return out


def ring_reduce(parts, axis, sent):
    size = SIZES[axis]
    me = lax.axis_index(axis)
    _, rows, cols = parts.shape
    half = cols // 2
    far = size // 2

    def get(offset, col):
        start = ((me + offset + size) % size, 0, col)
        return lax.dynamic_slice(parts, start, (1, rows, half))[0]

    right1, right2 = get(far, 0), get(far - 1, half)
    left1, left2 = get(1 - far, 0), get(-far, half)
    for step in range(1, far):
        right = jnp.concatenate((right1, right2), 1).astype(sent)
        left = jnp.concatenate((left1, left2), 1).astype(sent)
        right, left = lax.optimization_barrier((right, left))
        right = shift(right, axis, 1).astype(F32)
        left = shift(left, axis, -1).astype(F32)
        right1 = right[:, :half] + get(far - step, 0)
        left2 = left[:, half:] + get(step - far, half)
        if step < far - 1:
            right2 = right[:, half:] + get(far - 1 - step, half)
            left1 = left[:, :half] + get(step + 1 - far, 0)
        else:
            right2 = right[:, half:]
            left1 = left[:, :half]
    right1, left2 = lax.optimization_barrier((right1.astype(sent), left2.astype(sent)))
    right1 = shift(right1, axis, 1).astype(F32)
    left2 = shift(left2, axis, -1).astype(F32)
    return jnp.concatenate(
        (get(0, 0) + right1 + left1, get(0, half) + right2 + left2), 1
    )


def slot_maps(unit_order, rows_dev, groups, capacity, own):
    row = jnp.arange(rows_dev, dtype=jnp.int32)
    unit = jnp.arange(groups * rows_dev, dtype=jnp.int32)
    slot = jnp.arange(groups * capacity, dtype=jnp.int32)

    def slots_of(partner, rank_key):
        same = partner[:, None] == partner[None, :]
        before = rank_key[None, :] < rank_key[:, None]
        place = jnp.sum((same & before).astype(jnp.int32), axis=1)
        return partner * capacity + place

    found = unit_order[None, :] == (own * rows_dev + row)[:, None]
    user = jnp.sum(jnp.where(found, unit[None, :], 0), axis=1)
    send_slot = slots_of(user // rows_dev, user)
    mine = lax.dynamic_slice(unit_order, (own * rows_dev,), (rows_dev,))
    recv_slot = slots_of(mine // rows_dev, row)
    send_map = (slot[:, None] == send_slot[None, :]).astype(BF16)
    recv_map = (slot[:, None] == recv_slot[None, :]).astype(BF16)
    return send_map, recv_map


def near_gather(block, axis):
    size = SIZES[axis]
    me = lax.axis_index(axis)
    out = jnp.zeros((size,) + block.shape, block.dtype)
    for step in range(size):
        value = shift(block, axis, step) if step else block
        out = lax.dynamic_update_index_in_dim(out, value, (me - step + size) % size, 0)
    return out


def near_sum(parts, axis, sent):
    size = SIZES[axis]
    me = lax.axis_index(axis)
    total = lax.dynamic_index_in_dim(parts, me, 0, keepdims=False)
    for step in (1, size - 1, *range(2, size - 1)):
        term = lax.dynamic_index_in_dim(parts, (me + step) % size, 0, keepdims=False)
        total = total + shift(term.astype(sent), axis, step).astype(F32)
    return total


def exchange_sum(parts, axis):
    size = SIZES[axis]
    me = lax.axis_index(axis)
    got = lax.all_to_all(parts.astype(BF16), axis, split_axis=0, concat_axis=0, tiled=True)
    total = lax.dynamic_index_in_dim(parts, me, 0, keepdims=False)
    for i in range(size):
        total = total + jnp.where(me == i, 0.0, got[i].astype(F32))
    return total


def chip_sums(tokens, gate_up):
    core = lax.axis_index("c")
    half = tokens.shape[0] // 2
    give = lax.dynamic_slice_in_dim(tokens, (1 - core) * half, half, 0)
    keep = lax.dynamic_slice_in_dim(tokens, core * half, half, 0)
    taken = shift(product(give, gate_up, 1), "c", 1)
    partial = product(keep, gate_up, 1) + taken
    return partial


def unit_sums(partial, send_map, recv_map):
    units = send_map.shape[1]
    some = partial.shape[0] // SIZES["x"]
    sums = near_sum(partial.reshape(SIZES["x"], some, 4 * units), "x", BF16)
    first = jnp.concatenate((sums[:, :units], sums[:, units : 2 * units]), 0)
    second = jnp.concatenate((sums[:, 2 * units : 3 * units], sums[:, 3 * units :]), 0)
    out = jnp.concatenate(
        (product(send_map, second.astype(BF16), 1), product(recv_map, first.astype(BF16), 1)), 1
    ).astype(BF16)
    return out, (first, second)


def exchange_units(out, groups):
    parts = out.reshape(groups, -1, out.shape[1])
    got = lax.all_to_all(parts, ("z", "y"), split_axis=0, concat_axis=0, tiled=True)
    return got.reshape(out.shape)


def merged_hidden(got, sums, send_map, recv_map):
    first, second = sums
    some = first.shape[0] // 2
    core = lax.axis_index("c")
    half = SIZES["x"] * some
    units = send_map.shape[1]
    second_moved = product(got[:, : 2 * some], recv_map, 0)
    first_moved = product(got[:, 2 * some :], send_map, 0)

    def act(both):
        both = both * 0.5
        return (jax.nn.silu(both[:some]) * both[some:]).astype(BF16)

    hidden = jnp.concatenate((act(first + second_moved), act(first_moved + second)), 1)
    hidden = ring_gather(hidden, "x").reshape(half, 2 * units)
    other = shift(hidden, "c", 1)
    return jnp.where(
        core == 0,
        jnp.concatenate((hidden, other), 0),
        jnp.concatenate((other, hidden), 0),
    )


def local(
    tokens, gate_first, up_first, down_first, gate_second, up_second, down_second, unit_order
):
    rows_dev, width = gate_first.shape
    nz, ny = SIZES["z"], SIZES["y"]
    groups = nz * ny
    capacity = 2 * rows_dev // groups
    own = lax.axis_index("z") * ny + lax.axis_index("y")
    gate_up = jnp.concatenate((gate_first, up_first, gate_second, up_second), 0)
    down = jnp.concatenate((down_first, down_second), 0)
    send_map, recv_map = slot_maps(unit_order, rows_dev, groups, capacity, own)
    cut = 24
    rest = tokens.shape[0] - cut

    def by_y(rows):
        return rows.reshape(nz, ny, -1, rows.shape[-1]).transpose(1, 0, 2, 3).reshape(rows.shape)

    def output(hidden):
        return lax.dot(hidden, down, preferred_element_type=F32)

    near = near_gather(tokens[:cut], "y").reshape(ny * cut, width)
    near, late = lax.optimization_barrier((near, tokens[cut:]))
    every_early = lax.all_gather(near, "z", axis=0, tiled=True)
    late = jnp.broadcast_to(late[None], (nz, rest, width))
    late = lax.all_to_all(late, "z", split_axis=0, concat_axis=0, tiled=True)
    every_late = ring_gather(late.reshape(nz * rest, width), "y").reshape(-1, width)

    sent_late, sums_late = unit_sums(chip_sums(every_late, gate_up), send_map, recv_map)
    partial, sent_late = lax.optimization_barrier((chip_sums(every_early, gate_up), sent_late))
    sent_early, sums_early = unit_sums(partial, send_map, recv_map)
    got_late = exchange_units(sent_late, groups)
    got_early = exchange_units(sent_early, groups)
    hidden = merged_hidden(got_late, sums_late, send_map, recv_map)
    hidden = hidden.reshape(ny, nz, rest, -1).transpose(1, 0, 2, 3).reshape(groups * rest, -1)
    late, got_early = lax.optimization_barrier((output(hidden), got_early))
    late = exchange_sum(late.reshape(nz, ny * rest, width), "z")

    hidden = by_y(merged_hidden(got_early, sums_early, send_map, recv_map))
    early = ring_reduce(output(hidden).reshape(ny, nz * cut, width), "y", BF16)
    early = exchange_sum(early.reshape(nz, cut, width), "z")
    late = near_sum(late.reshape(ny, rest, width), "y", F32)
    return (jnp.concatenate((early, late), 0) * 0.5).astype(BF16)


def solution(mesh):
    fine = Mesh(mesh.devices.reshape(tuple(SIZES.values())), tuple(SIZES))
    block = P(("z", "y"), ("x", "c"))
    return jax.shard_map(
        local, mesh=fine, in_specs=(block,) * 7 + (P(),), out_specs=block, check_vma=False
    )
```

```python
import jax
import jax.numpy as jnp
from jax import lax
from jax.sharding import Mesh, PartitionSpec as P

F32 = jnp.float32
BF16 = jnp.bfloat16
SIZES = {"z": 8, "y": 4, "x": 4, "c": 2}


def product(left, right, axis):
    return lax.dot_general(left, right, (((axis,), (axis,)), ((), ())), preferred_element_type=F32)


def shift(value, axis, step):
    size = SIZES[axis]
    return lax.ppermute(value, axis, [(i, (i + step) % size) for i in range(size)])


def ring_gather(block, axis):
    size = SIZES[axis]
    me = lax.axis_index(axis)
    rows, cols = block.shape
    out = jnp.zeros((size, rows, cols), block.dtype)

    def put(out, value, offset, col):
        return lax.dynamic_update_slice(out, value[None], ((me + offset + size) % size, 0, col))

    out = put(out, block, 0, 0)
    right = left = block
    for step in range(1, size // 2):
        right = shift(right, axis, 1)
        left = shift(left, axis, -1)
        out = put(out, right, -step, 0)
        out = put(out, left, step, 0)
    half = cols // 2
    first = shift(right[:, :half], axis, 1)
    second = shift(left[:, half:], axis, -1)
    out = put(out, first, size // 2, 0)
    out = put(out, second, size // 2, half)
    return out


def ring_reduce(parts, axis, sent):
    size = SIZES[axis]
    me = lax.axis_index(axis)
    _, rows, cols = parts.shape
    half = cols // 2
    far = size // 2

    def get(offset, col):
        start = ((me + offset + size) % size, 0, col)
        return lax.dynamic_slice(parts, start, (1, rows, half))[0]

    right1, right2 = get(far, 0), get(far - 1, half)
    left1, left2 = get(1 - far, 0), get(-far, half)
    for step in range(1, far):
        right = jnp.concatenate((right1, right2), 1).astype(sent)
        left = jnp.concatenate((left1, left2), 1).astype(sent)
        right, left = lax.optimization_barrier((right, left))
        right = shift(right, axis, 1).astype(F32)
        left = shift(left, axis, -1).astype(F32)
        right1 = right[:, :half] + get(far - step, 0)
        left2 = left[:, half:] + get(step - far, half)
        if step < far - 1:
            right2 = right[:, half:] + get(far - 1 - step, half)
            left1 = left[:, :half] + get(step + 1 - far, 0)
        else:
            right2 = right[:, half:]
            left1 = left[:, :half]
    right1, left2 = lax.optimization_barrier((right1.astype(sent), left2.astype(sent)))
    right1 = shift(right1, axis, 1).astype(F32)
    left2 = shift(left2, axis, -1).astype(F32)
    return jnp.concatenate(
        (get(0, 0) + right1 + left1, get(0, half) + right2 + left2), 1
    )


def slot_tables(unit_order, rows_dev, groups, capacity, own):
    row = jnp.arange(rows_dev, dtype=jnp.int32)
    unit = jnp.arange(groups * rows_dev, dtype=jnp.int32)

    def slots_of(partner, rank_key):
        same = partner[:, None] == partner[None, :]
        before = rank_key[None, :] < rank_key[:, None]
        place = jnp.sum((same & before).astype(jnp.int32), axis=1)
        return partner * capacity + place

    found = unit_order[None, :] == (own * rows_dev + row)[:, None]
    user = jnp.sum(jnp.where(found, unit[None, :], 0), axis=1)
    mine = lax.dynamic_slice(unit_order, (own * rows_dev,), (rows_dev,))
    return slots_of(user // rows_dev, user), slots_of(mine // rows_dev, row)


def slot_map(slots, count):
    return (jnp.arange(count, dtype=jnp.int32)[:, None] == slots[None, :]).astype(BF16)


def near_gather(block, axis):
    size = SIZES[axis]
    me = lax.axis_index(axis)
    out = jnp.zeros((size,) + block.shape, block.dtype)
    for step in range(size):
        value = shift(block, axis, step) if step else block
        out = lax.dynamic_update_index_in_dim(out, value, (me - step + size) % size, 0)
    return out


def near_sum(parts, axis, sent):
    size = SIZES[axis]
    me = lax.axis_index(axis)
    total = lax.dynamic_index_in_dim(parts, me, 0, keepdims=False)
    for step in (1, size - 1, *range(2, size - 1)):
        term = lax.dynamic_index_in_dim(parts, (me + step) % size, 0, keepdims=False)
        total = total + shift(term.astype(sent), axis, step).astype(F32)
    return total


def exchange_sum(parts, axis):
    size = SIZES[axis]
    me = lax.axis_index(axis)
    got = lax.all_to_all(parts.astype(BF16), axis, split_axis=0, concat_axis=0, tiled=True)
    total = lax.dynamic_index_in_dim(parts, me, 0, keepdims=False)
    for i in range(size):
        total = total + jnp.where(me == i, 0.0, got[i].astype(F32))
    return total


def chip_sums(tokens, gate_up):
    core = lax.axis_index("c")
    half = tokens.shape[0] // 2
    give = lax.dynamic_slice_in_dim(tokens, (1 - core) * half, half, 0)
    keep = lax.dynamic_slice_in_dim(tokens, core * half, half, 0)
    taken = shift(product(give, gate_up, 1), "c", 1)
    partial = product(keep, gate_up, 1) + taken
    return partial


def unit_sums(partial, send_map, recv_map):
    units = send_map.shape[1]
    some = partial.shape[0] // SIZES["x"]
    sums = near_sum(partial.reshape(SIZES["x"], some, 4 * units), "x", BF16)
    first = jnp.concatenate((sums[:, :units], sums[:, units : 2 * units]), 0)
    second = jnp.concatenate((sums[:, 2 * units : 3 * units], sums[:, 3 * units :]), 0)
    out = jnp.concatenate(
        (product(send_map, second.astype(BF16), 1), product(recv_map, first.astype(BF16), 1)), 1
    ).astype(BF16)
    return out, (first, second)


def exchange_units(out, groups):
    parts = out.reshape(groups, -1, out.shape[1])
    got = lax.all_to_all(parts, ("z", "y"), split_axis=0, concat_axis=0, tiled=True)
    return got.reshape(out.shape)


def merged_hidden(got, sums, send_map, recv_map):
    first, second = sums
    some = first.shape[0] // 2
    core = lax.axis_index("c")
    half = SIZES["x"] * some
    units = send_map.shape[1]
    second_moved = product(got[:, : 2 * some], recv_map, 0)
    first_moved = product(got[:, 2 * some :], send_map, 0)

    def act(both):
        both = both * 0.5
        return (jax.nn.silu(both[:some]) * both[some:]).astype(BF16)

    hidden = jnp.concatenate((act(first + second_moved), act(first_moved + second)), 1)
    hidden = ring_gather(hidden, "x").reshape(half, 2 * units)
    other = shift(hidden, "c", 1)
    return jnp.where(
        core == 0,
        jnp.concatenate((hidden, other), 0),
        jnp.concatenate((other, hidden), 0),
    )


def local(
    tokens, gate_first, up_first, down_first, gate_second, up_second, down_second, unit_order
):
    rows_dev, width = gate_first.shape
    nz, ny = SIZES["z"], SIZES["y"]
    groups = nz * ny
    capacity = 2 * rows_dev // groups
    own = lax.axis_index("z") * ny + lax.axis_index("y")
    gate_up = jnp.concatenate((gate_first, up_first, gate_second, up_second), 0)
    down = jnp.concatenate((down_first, down_second), 0)
    slots = slot_tables(unit_order, rows_dev, groups, capacity, own)
    cut = 24
    rest = tokens.shape[0] - cut

    def by_y(rows):
        return rows.reshape(nz, ny, -1, rows.shape[-1]).transpose(1, 0, 2, 3).reshape(rows.shape)

    def output(hidden):
        return lax.dot(hidden, down, preferred_element_type=F32)

    near = near_gather(tokens[:cut], "y").reshape(ny * cut, width)
    near, late = lax.optimization_barrier((near, tokens[cut:]))
    every_early = lax.all_gather(near, "z", axis=0, tiled=True)
    late = jnp.broadcast_to(late[None], (nz, rest, width))
    late = lax.all_to_all(late, "z", split_axis=0, concat_axis=0, tiled=True)
    late, slots = lax.optimization_barrier((late, slots))
    send_map = slot_map(slots[0], groups * capacity)
    recv_map = slot_map(slots[1], groups * capacity)
    every_late = ring_gather(late.reshape(nz * rest, width), "y").reshape(-1, width)

    sent_late, sums_late = unit_sums(chip_sums(every_late, gate_up), send_map, recv_map)
    partial, sent_late = lax.optimization_barrier((chip_sums(every_early, gate_up), sent_late))
    sent_early, sums_early = unit_sums(partial, send_map, recv_map)
    got_late = exchange_units(sent_late, groups)
    got_early = exchange_units(sent_early, groups)
    hidden = merged_hidden(got_late, sums_late, send_map, recv_map)
    hidden = hidden.reshape(ny, nz, rest, -1).transpose(1, 0, 2, 3).reshape(groups * rest, -1)
    late, got_early = lax.optimization_barrier((output(hidden), got_early))
    late = lax.psum_scatter(late.reshape(nz * ny * rest, width), "z", scatter_dimension=0, tiled=True)

    hidden = by_y(merged_hidden(got_early, sums_early, send_map, recv_map))
    early = ring_reduce(output(hidden).reshape(ny, nz * cut, width), "y", BF16)
    early = exchange_sum(early.reshape(nz, cut, width), "z")
    late = near_sum(late.reshape(ny, rest, width), "y", F32)
    return (jnp.concatenate((early, late), 0) * 0.5).astype(BF16)


def solution(mesh):
    fine = Mesh(mesh.devices.reshape(tuple(SIZES.values())), tuple(SIZES))
    block = P(("z", "y"), ("x", "c"))
    return jax.shard_map(
        local, mesh=fine, in_specs=(block,) * 7 + (P(),), out_specs=block, check_vma=False
    )
```

```python
import jax
import jax.numpy as jnp
from jax import lax
from jax.sharding import Mesh, PartitionSpec as P

F32 = jnp.float32
BF16 = jnp.bfloat16
SIZES = {"z": 8, "y": 4, "x": 4, "c": 2}


def product(left, right, axis):
    return lax.dot_general(left, right, (((axis,), (axis,)), ((), ())), preferred_element_type=F32)


def shift(value, axis, step):
    size = SIZES[axis]
    return lax.ppermute(value, axis, [(i, (i + step) % size) for i in range(size)])


def ring_gather(block, axis):
    size = SIZES[axis]
    me = lax.axis_index(axis)
    rows, cols = block.shape
    out = jnp.zeros((size, rows, cols), block.dtype)

    def put(out, value, offset, col):
        return lax.dynamic_update_slice(out, value[None], ((me + offset + size) % size, 0, col))

    out = put(out, block, 0, 0)
    right = left = block
    for step in range(1, size // 2):
        right = shift(right, axis, 1)
        left = shift(left, axis, -1)
        out = put(out, right, -step, 0)
        out = put(out, left, step, 0)
    half = cols // 2
    first = shift(right[:, :half], axis, 1)
    second = shift(left[:, half:], axis, -1)
    out = put(out, first, size // 2, 0)
    out = put(out, second, size // 2, half)
    return out


def ring_reduce(parts, axis, sent):
    size = SIZES[axis]
    me = lax.axis_index(axis)
    _, rows, cols = parts.shape
    half = cols // 2
    far = size // 2

    def get(offset, col):
        start = ((me + offset + size) % size, 0, col)
        return lax.dynamic_slice(parts, start, (1, rows, half))[0]

    right1, right2 = get(far, 0), get(far - 1, half)
    left1, left2 = get(1 - far, 0), get(-far, half)
    for step in range(1, far):
        right = jnp.concatenate((right1, right2), 1).astype(sent)
        left = jnp.concatenate((left1, left2), 1).astype(sent)
        right, left = lax.optimization_barrier((right, left))
        right = shift(right, axis, 1).astype(F32)
        left = shift(left, axis, -1).astype(F32)
        right1 = right[:, :half] + get(far - step, 0)
        left2 = left[:, half:] + get(step - far, half)
        if step < far - 1:
            right2 = right[:, half:] + get(far - 1 - step, half)
            left1 = left[:, :half] + get(step + 1 - far, 0)
        else:
            right2 = right[:, half:]
            left1 = left[:, :half]
    right1, left2 = lax.optimization_barrier((right1.astype(sent), left2.astype(sent)))
    right1 = shift(right1, axis, 1).astype(F32)
    left2 = shift(left2, axis, -1).astype(F32)
    return jnp.concatenate(
        (get(0, 0) + right1 + left1, get(0, half) + right2 + left2), 1
    )


def slot_tables(unit_order, rows_dev, groups, capacity, own):
    row = jnp.arange(rows_dev, dtype=jnp.int32)
    unit = jnp.arange(groups * rows_dev, dtype=jnp.int32)

    def slots_of(partner, rank_key):
        same = partner[:, None] == partner[None, :]
        before = rank_key[None, :] < rank_key[:, None]
        place = jnp.sum((same & before).astype(jnp.int32), axis=1)
        return partner * capacity + place

    found = unit_order[None, :] == (own * rows_dev + row)[:, None]
    user = jnp.sum(jnp.where(found, unit[None, :], 0), axis=1)
    mine = lax.dynamic_slice(unit_order, (own * rows_dev,), (rows_dev,))
    return slots_of(user // rows_dev, user), slots_of(mine // rows_dev, row)


def slot_map(slots, count):
    return (jnp.arange(count, dtype=jnp.int32)[:, None] == slots[None, :]).astype(BF16)


def near_gather(block, axis):
    size = SIZES[axis]
    me = lax.axis_index(axis)
    out = jnp.zeros((size,) + block.shape, block.dtype)
    for step in range(size):
        value = shift(block, axis, step) if step else block
        out = lax.dynamic_update_index_in_dim(out, value, (me - step + size) % size, 0)
    return out


def near_sum(parts, axis, sent):
    size = SIZES[axis]
    me = lax.axis_index(axis)
    total = lax.dynamic_index_in_dim(parts, me, 0, keepdims=False)
    for step in (1, size - 1, *range(2, size - 1)):
        term = lax.dynamic_index_in_dim(parts, (me + step) % size, 0, keepdims=False)
        total = total + shift(term.astype(sent), axis, step).astype(F32)
    return total


def exchange_sum(parts, axis):
    size = SIZES[axis]
    me = lax.axis_index(axis)
    got = lax.all_to_all(parts.astype(BF16), axis, split_axis=0, concat_axis=0, tiled=True)
    total = lax.dynamic_index_in_dim(parts, me, 0, keepdims=False)
    for i in range(size):
        total = total + jnp.where(me == i, 0.0, got[i].astype(F32))
    return total


def chip_sums(tokens, gate_up):
    core = lax.axis_index("c")
    half = tokens.shape[0] // 2
    give = lax.dynamic_slice_in_dim(tokens, (1 - core) * half, half, 0)
    keep = lax.dynamic_slice_in_dim(tokens, core * half, half, 0)
    taken = shift(product(give, gate_up, 1), "c", 1)
    partial = product(keep, gate_up, 1) + taken
    return partial


def unit_sums(partial, send_map, recv_map):
    units = send_map.shape[1]
    some = partial.shape[0] // SIZES["x"]
    sums = near_sum(partial.reshape(SIZES["x"], some, 4 * units), "x", BF16)
    first = jnp.concatenate((sums[:, :units], sums[:, units : 2 * units]), 0)
    second = jnp.concatenate((sums[:, 2 * units : 3 * units], sums[:, 3 * units :]), 0)
    out = jnp.concatenate(
        (product(send_map, second.astype(BF16), 1), product(recv_map, first.astype(BF16), 1)), 1
    ).astype(BF16)
    return out, (first, second)


def exchange_units(out, groups):
    parts = out.reshape(groups, -1, out.shape[1])
    got = lax.all_to_all(parts, ("z", "y"), split_axis=0, concat_axis=0, tiled=True)
    return got.reshape(out.shape)


def merged_hidden(got, sums, send_map, recv_map):
    first, second = sums
    some = first.shape[0] // 2
    core = lax.axis_index("c")
    half = SIZES["x"] * some
    units = send_map.shape[1]
    second_moved = product(got[:, : 2 * some], recv_map, 0)
    first_moved = product(got[:, 2 * some :], send_map, 0)

    def act(both):
        both = both * 0.5
        return (jax.nn.silu(both[:some]) * both[some:]).astype(BF16)

    hidden = jnp.concatenate((act(first + second_moved), act(first_moved + second)), 1)
    hidden = ring_gather(hidden, "x").reshape(half, 2 * units)
    other = shift(hidden, "c", 1)
    return jnp.where(
        core == 0,
        jnp.concatenate((hidden, other), 0),
        jnp.concatenate((other, hidden), 0),
    )


def local(
    tokens, gate_first, up_first, down_first, gate_second, up_second, down_second, unit_order
):
    rows_dev, width = gate_first.shape
    nz, ny = SIZES["z"], SIZES["y"]
    groups = nz * ny
    capacity = 2 * rows_dev // groups
    own = lax.axis_index("z") * ny + lax.axis_index("y")
    cut = 24
    rest = tokens.shape[0] - cut

    def by_y(rows):
        return rows.reshape(nz, ny, -1, rows.shape[-1]).transpose(1, 0, 2, 3).reshape(rows.shape)

    def output(hidden):
        return lax.dot(hidden, down, preferred_element_type=F32)

    near = near_gather(tokens[:cut], "y").reshape(ny * cut, width)
    near, late, unit_order, gate_first, down_first = lax.optimization_barrier(
        (near, tokens[cut:], unit_order, gate_first, down_first)
    )
    gate_up = jnp.concatenate((gate_first, up_first, gate_second, up_second), 0)
    down = jnp.concatenate((down_first, down_second), 0)
    slots = slot_tables(unit_order, rows_dev, groups, capacity, own)
    every_early = lax.all_gather(near, "z", axis=0, tiled=True)
    late = ring_gather(late, "z")
    late, slots = lax.optimization_barrier((late, slots))
    send_map = slot_map(slots[0], groups * capacity)
    recv_map = slot_map(slots[1], groups * capacity)
    every_late = ring_gather(late.reshape(nz * rest, width), "y").reshape(-1, width)

    sent_late, sums_late = unit_sums(chip_sums(every_late, gate_up), send_map, recv_map)
    partial, sent_late = lax.optimization_barrier((chip_sums(every_early, gate_up), sent_late))
    sent_early, sums_early = unit_sums(partial, send_map, recv_map)
    got_late = exchange_units(sent_late, groups)
    got_early = exchange_units(sent_early, groups)
    hidden = merged_hidden(got_late, sums_late, send_map, recv_map)
    hidden = hidden.reshape(ny, nz, rest, -1).transpose(1, 0, 2, 3).reshape(groups * rest, -1)
    late, got_early = lax.optimization_barrier((output(hidden), got_early))
    late = lax.psum_scatter(late.reshape(nz * ny * rest, width), "z", scatter_dimension=0, tiled=True)

    hidden = by_y(merged_hidden(got_early, sums_early, send_map, recv_map))
    early = ring_reduce(output(hidden).reshape(ny, nz * cut, width), "y", BF16)
    early = exchange_sum(early.reshape(nz, cut, width), "z")
    late = near_sum(late.reshape(ny, rest, width), "y", F32)
    return (jnp.concatenate((early, late), 0) * 0.5).astype(BF16)


def solution(mesh):
    fine = Mesh(mesh.devices.reshape(tuple(SIZES.values())), tuple(SIZES))
    block = P(("z", "y"), ("x", "c"))
    return jax.shard_map(
        local, mesh=fine, in_specs=(block,) * 7 + (P(),), out_specs=block, check_vma=False
    )
```
